256 devices in a mesh: seq: 32 (over y, x, core), mp: 8 (over z).
Axes of the slice: x: 4, y: 4, z: 8, core: 2. Of those that a mesh axis runs over, the one named last changes fastest.
Arguments:
- span_states: bfloat16 [4096, 4096], P('seq'), may hold values from -6 to 6
- dec_query: bfloat16 [4096, 2048], P('seq', 'mp'), may hold values from -256 to 256
- nbr_query: bfloat16 [256, 128, 2048], P('seq', None, 'mp'), may hold values from -256 to 256
- nbr_index: int32 [64, 4], P('seq'), may hold values from 0 to 255, as said below
- nbr_count: int32 [64], P('seq'), may hold values from 2 to 4
- wkv_enc: bfloat16 [4096, 2, 2048], P(None, None, 'mp'), may hold values from -0.09375 to 0.09375
- wo_enc: bfloat16 [2048, 4096], P('mp'), may hold values from -0.125 to 0.125
- wkv_dec: bfloat16 [4096, 2, 2048], P(None, None, 'mp'), may hold values from -0.09375 to 0.09375
- grad_out: bfloat16 [4096, 4096], P('seq'), may hold values from -6 to 6
Outputs:
- attended: bfloat16 [4096, 2048], P('seq', 'mp')
- grad_wo: float32 [2048, 4096], P('mp', 'seq')
The draws below stay inside these ranges and needn't reach their ends.
Inputs may be any that keep to these rules, and one draw needn't show every extreme that they name: `nbr_index`: every row of nbr_query is named exactly once. The entries of the spans of one device name rows in exactly 8 distinct aligned blocks of 8 rows, 1 in each. Entries of slots k >= nbr_count[c] name rows that are not used.
All inputs are finite; a program needn't handle non-finite values.
Results may differ from the reference program's by a relative error of at most 0.025.
Values may be sent and summed in bfloat16 or wider, within the bound.
No kernel may reach another device: no remote copies, remote signals or barrier semaphores. Data moves between devices by JAX's collectives and lax.ppermute only.
A program may use at most 128 MiB of HBM per device.

```python
import math
import jax
import jax.numpy as jnp
from jax import lax

D = 4096
HEADS = 16
DH = 128
CLEN = 64
NLEN = 128
KMAX = 4
SPANS_DEV = 2
HW = 2048
SPANS = 64
TOKENS = 4096
NBRS = 256
N_MP = 8


def draw_nbr_index(key, part):
    key = jax.random.fold_in(key, 11)
    devices_seq = SPANS // SPANS_DEV
    slot_total = SPANS_DEV * KMAX
    capacity = max(1, slot_total // devices_seq)
    groups = slot_total // capacity
    relabel_key, shift_key, offset_key, order_key = jax.random.split(key, 4)
    relabel = jax.random.permutation(relabel_key, devices_seq)
    shifted = jax.random.permutation(shift_key, devices_seq)
    offsets = jax.random.permutation(offset_key, devices_seq)[:groups]
    sorted_orders = jax.vmap(lambda sub: jax.random.permutation(sub, slot_total))(jax.random.split(order_key, devices_seq))
    homes = relabel[(shifted[:, None] + offsets[sorted_orders // capacity]) % devices_seq]
    rows = homes * slot_total + sorted_orders
    return rows.reshape(SPANS, KMAX).astype(jnp.int32)


def draw_nbr_count(key, part):
    key = jax.random.fold_in(key, 12)
    value_key, low_key, high_key = jax.random.split(key, 3)
    counts = jax.random.randint(value_key, (SPANS,), 2, KMAX + 1)
    low_spot = jax.random.randint(low_key, (), 0, SPANS)
    high_spot = (low_spot + 1 + jax.random.randint(high_key, (), 0, SPANS - 1)) % SPANS
    counts = counts.at[low_spot].set(2).at[high_spot].set(KMAX)
    return counts.astype(jnp.int32)


def draw_dec_query(key, part):
    key = jax.random.fold_in(key, 31)
    drawn_key = jax.random.fold_in(key, 0)
    return (2.0 * jnp.clip(jax.random.normal(drawn_key, (TOKENS, HW), jnp.float32), -6.0, 6.0)).astype(jnp.bfloat16)


def draw_nbr_query(key, part):
    key = jax.random.fold_in(key, 41)
    drawn_key = jax.random.fold_in(key, 0)
    return jnp.clip(jax.random.normal(drawn_key, (NBRS, NLEN, HW), jnp.float32), -6.0, 6.0).astype(jnp.bfloat16)


def with_spikes(entries, stream_key, source, target, blocks, factor):
    def block_of(position):
        return (jnp.arange(entries.shape[position]) // (entries.shape[position] // blocks)).reshape((-1,) + (1,) * (entries.ndim - 1 - position))

    first = jax.random.permutation(stream_key, blocks)[block_of(target)]
    far = (block_of(target) + blocks // 2) % blocks
    return jnp.where((block_of(source) == first) | (block_of(source) == far), factor * entries, entries)


def levels(key, dims, cuts, least, largest):
    factor_of = 1.0
    for dim, shards_of in cuts:
        heights = jax.random.uniform(jax.random.fold_in(jax.random.fold_in(key, 6), dim), (shards_of,), jnp.float32, least / len(cuts), largest / len(cuts))
        factor_of = factor_of * jnp.repeat(jnp.exp(heights), dims[dim] // shards_of).reshape((-1,) + (1,) * (len(dims) - 1 - dim))
    return factor_of


def normal_values(own_key, dims, scale, bound, cuts=(), kind=jnp.bfloat16):
    drawn = scale * jax.random.normal(own_key, dims, jnp.float32)
    if cuts:
        drawn = drawn * levels(own_key, dims, cuts, -0.22, 0.18)
    return jnp.clip(drawn, -bound, bound).astype(kind)


def gaussian_with(key, dims, scale, limit, pieces, heavy, kind=jnp.bfloat16):
    values = scale * jax.random.normal(key, dims, jnp.float32)
    if pieces:
        values = values * levels(key, dims, pieces, -0.22, 0.18)
    return jnp.clip(with_spikes(values, jax.random.fold_in(key, 3), *heavy), -limit, limit).astype(kind)


def setup_inputs(seed: int = 0) -> dict:
    key_list = jax.random.split(jax.random.key(seed), 10)
    return {
        "span_states": normal_values(key_list[0], (TOKENS, D), 1.0, 6.0, ((0, 32),)),
        "dec_query": draw_dec_query(jax.random.fold_in(key_list[9], 71), 0),
        "nbr_query": draw_nbr_query(jax.random.fold_in(key_list[9], 71), 0),
        "nbr_index": draw_nbr_index(jax.random.fold_in(key_list[9], 71), 0),
        "nbr_count": draw_nbr_count(jax.random.fold_in(key_list[9], 71), 0),
        "wkv_enc": normal_values(key_list[5], (D, 2, HW), D ** -0.5, 0.09375, ((2, 8),)),
        "wo_enc": normal_values(key_list[6], (HW, D), HW ** -0.5, 0.125, ((0, 8),)),
        "wkv_dec": normal_values(key_list[7], (D, 2, HW), D ** -0.5, 0.09375, ((2, 8),)),
        "grad_out": gaussian_with(key_list[8], (TOKENS, D), 1.0, 6.0, ((0, 32),), (0, 1, 32, 2.75)),
    }


def normalize(scores, usable):
    scores = jnp.where(usable, scores, -1e+30)
    highest = lax.optimization_barrier(jnp.max(scores, axis=-1, keepdims=True))
    exponent = jnp.exp(scores - highest)
    return (exponent / lax.optimization_barrier(jnp.sum(exponent, axis=-1, keepdims=True))).astype(jnp.bfloat16)

def reference(span_states, dec_query, nbr_query, nbr_index, nbr_count, wkv_enc, wo_enc, wkv_dec, grad_out):
    enc_pairs = jnp.dot(span_states, wkv_enc.reshape(D, 2 * HW), preferred_element_type=jnp.float32).astype(jnp.bfloat16)
    group_width = HW // N_MP
    output_groups = wo_enc.reshape(N_MP, group_width, D).astype(jnp.float32)
    dec_matrix = wkv_dec.reshape(D, 2 * HW)

    def one_span(span_id):
        pairs = lax.dynamic_slice_in_dim(enc_pairs, span_id * CLEN, CLEN, 0).reshape(CLEN, 2, HEADS, DH)
        queries = nbr_query[nbr_index[span_id]].reshape(KMAX, NLEN, HEADS, DH)
        scores = jnp.einsum('knhd,lhd->khnl', queries.astype(jnp.float32), pairs[:, 0].astype(jnp.float32)) / math.sqrt(DH)
        weights = normalize(scores, True)
        heads_out = jnp.einsum('khnl,lhd->knhd', weights.astype(jnp.float32), pairs[:, 1].astype(jnp.float32)).astype(jnp.bfloat16)
        grouped_rows = heads_out.reshape(KMAX * NLEN, N_MP, group_width).astype(jnp.float32)
        part_list = jnp.einsum('ljs,jse->jle', grouped_rows, output_groups)
        encoded = lax.optimization_barrier(jnp.sum(part_list, axis=0)).astype(jnp.bfloat16)
        dec_pairs = jnp.dot(encoded, dec_matrix, preferred_element_type=jnp.float32).astype(jnp.bfloat16)
        dec_pairs = dec_pairs.reshape(KMAX * NLEN, 2, HEADS, DH)
        span_query = lax.dynamic_slice_in_dim(dec_query, span_id * CLEN, CLEN, 0).reshape(CLEN, HEADS, DH)
        dec_scores = jnp.einsum('lhd,jhd->hlj', span_query.astype(jnp.float32), dec_pairs[:, 0].astype(jnp.float32)) / math.sqrt(DH)
        usable = (jnp.arange(KMAX * NLEN, dtype=jnp.int32) // NLEN < nbr_count[span_id])[None, None, :]
        dec_weights = normalize(dec_scores, usable)
        result = jnp.einsum('hlj,jhd->lhd', dec_weights.astype(jnp.float32), dec_pairs[:, 1].astype(jnp.float32))
        return result.astype(jnp.bfloat16).reshape(CLEN, HW)
    attended = lax.map(one_span, jnp.arange(SPANS, dtype=jnp.int32)).reshape(TOKENS, HW)
    grad_wo = jnp.dot(attended.T, grad_out, preferred_element_type=jnp.float32)
    return (attended, grad_wo)
```

```python
import functools
import math

import jax
import jax.numpy as jnp
from jax import lax
from jax.experimental import pallas as pl
from jax.experimental.pallas import tpu as pltpu
from jax.sharding import PartitionSpec as P

DH = 128
BF = jnp.bfloat16
F32 = jnp.float32
VMEM = pl.BlockSpec(memory_space=pltpu.VMEM)
SMEM = pl.BlockSpec(memory_space=pltpu.SMEM)
ANY = pl.BlockSpec(memory_space=pl.ANY)
NT = (((1,), (1,)), ((), ()))


def params():
    return pltpu.CompilerParams(vmem_limit_bytes=32 * 1024 * 1024)


def outbox_kernel(tags, query, out0, out1, sems):
    count = out0.shape[0]

    def copies(dest):
        row = tags[dest] - 1
        return [
            pltpu.make_async_copy(
                query.at[row, :, pl.ds(h * DH, DH)], out.at[dest], sems.at[h, dest]
            )
            for h, out in enumerate((out0, out1))
        ]

    for dest in range(count):

        @pl.when(tags[dest] > 0)
        def _():
            for copy in copies(dest):
                copy.start()

    for dest in range(count):

        @pl.when(tags[dest] > 0)
        def _():
            for copy in copies(dest):
                copy.wait()


def outbox(tags, query, buckets):
    rows, length, width = query.shape
    shape = jax.ShapeDtypeStruct((buckets, length, DH), BF)
    return pl.pallas_call(
        outbox_kernel,
        out_shape=(shape, shape),
        in_specs=[SMEM, ANY],
        out_specs=(ANY, ANY),
        scratch_shapes=[pltpu.SemaphoreType.DMA((2, buckets))],
        compiler_params=params(),
    )(tags, query)


def encode_kernel(head, rows, index, inbox, pairs, out, held, sems):
    spans, slots = index.shape
    span_len = pairs.shape[0] // spans
    copies = []
    for j in range(spans * slots):
        home = index[j // slots, j % slots] // rows
        copies.append(pltpu.make_async_copy(inbox.at[home], held.at[j], sems.at[j]))
        copies[-1].start()
    for j in range(spans * slots):
        c, k = j // slots, j % slots
        copies[j].wait()
        keys = pairs[c * span_len : (c + 1) * span_len, head * DH : (head + 1) * DH]
        scores = lax.dot_general(keys, held[j], NT, preferred_element_type=F32) / math.sqrt(DH)
        exponent = jnp.exp(scores - jnp.max(scores, axis=0, keepdims=True))
        weights = exponent / jnp.sum(exponent, axis=0, keepdims=True)
        out[c * span_len : (c + 1) * span_len, k * DH : (k + 1) * DH] = weights.astype(BF)


def encode(head, index, inbox, pairs):
    spans, slots = index.shape
    return pl.pallas_call(
        functools.partial(encode_kernel, head, spans * slots),
        out_shape=jax.ShapeDtypeStruct((pairs.shape[0], slots * inbox.shape[1]), BF),
        in_specs=[SMEM, ANY, VMEM],
        out_specs=VMEM,
        scratch_shapes=[
            pltpu.VMEM((spans * slots,) + inbox.shape[1:], BF),
            pltpu.SemaphoreType.DMA((spans * slots,)),
        ],
        compiler_params=params(),
    )(index, inbox, pairs)


def fold_kernel(place, values, mine, other, out):
    groups = values.shape[0]
    spans = out.shape[0]
    span_len = values.shape[1] // spans
    z, core = place[0], place[1]
    for rel in range(groups):
        g = lax.rem(z + rel, groups)
        own = mine[g]
        far = other[g]
        first = jnp.where(core == 0, own, far)
        second = jnp.where(core == 0, far, own)
        low = jnp.dot(values[g, :, :DH], first, preferred_element_type=F32)
        high = jnp.dot(values[g, :, DH:], second, preferred_element_type=F32)
        for c in range(spans):
            at = slice(c * span_len, (c + 1) * span_len)
            both = jnp.concatenate([low[at], high[at]], axis=0)
            out[c, :, rel * 2 * span_len : (rel + 1) * 2 * span_len] = both.T.astype(BF)


def fold(place, values, mine, other, spans):
    groups, tokens, _ = values.shape
    width = mine.shape[2]
    return pl.pallas_call(
        fold_kernel,
        out_shape=jax.ShapeDtypeStruct((spans, width, groups * 2 * tokens // spans), BF),
        in_specs=[SMEM, VMEM, VMEM, VMEM],
        out_specs=VMEM,
        compiler_params=params(),
    )(place, values, mine, other)


def decode_kernel(place, counts, folded, query, *refs):
    spans = folded.shape[0]
    span_len = query.shape[0] // spans
    pieces, (out, send, held, sems) = refs[:-4], refs[-4:]
    copies = []
    for c in range(spans):
        row = []
        for i, piece in enumerate(pieces):
            row.append(
                pltpu.make_async_copy(
                    piece.at[pl.ds(c * span_len, span_len)],
                    held.at[c, pl.ds(i * span_len, span_len)],
                    sems.at[c, i],
                )
            )
            row[-1].start()
        copies.append(row)
    slot_tokens = held.shape[2]
    for c in range(spans):
        for copy in copies[c]:
            copy.wait()
        both = jnp.dot(folded[c], held[c], preferred_element_type=F32).astype(BF)
        usable = lax.broadcasted_iota(jnp.int32, (span_len, slot_tokens), 1) < counts[c] * DH
        for h in range(2):
            at = slice(c * span_len, (c + 1) * span_len)
            keys = both[h * DH : (h + 1) * DH]
            values = both[(2 + h) * DH : (3 + h) * DH]
            scores = jnp.dot(
                query[at, h * DH : (h + 1) * DH], keys, preferred_element_type=F32
            ) / math.sqrt(DH)
            scores = jnp.where(usable, scores, -1e30)
            exponent = jnp.exp(scores - jnp.max(scores, axis=1, keepdims=True))
            weights = (exponent / jnp.sum(exponent, axis=1, keepdims=True)).astype(BF)
            result = lax.dot_general(weights, values, NT, preferred_element_type=F32)
            out[at, h * DH : (h + 1) * DH] = result.astype(BF)
    send[...] = jnp.where(place[1] == 0, out[:, DH:], out[:, :DH])


def decode(place, counts, folded, query, pieces):
    spans = folded.shape[0]
    tokens, width = query.shape
    return pl.pallas_call(
        decode_kernel,
        out_shape=(
            jax.ShapeDtypeStruct((tokens, width), BF),
            jax.ShapeDtypeStruct((tokens, DH), BF),
        ),
        in_specs=[SMEM, SMEM, VMEM, VMEM] + [ANY] * len(pieces),
        out_specs=(VMEM, VMEM),
        scratch_shapes=[
            pltpu.VMEM((spans, folded.shape[2], pieces[0].shape[1]), BF),
            pltpu.SemaphoreType.DMA((spans, len(pieces))),
        ],
        compiler_params=params(),
    )(place, counts, folded, query, *pieces)


def partial_kernel(place, attended, near, grad, near_grad, out):
    own = jnp.where(place[1] == 0, attended[:, :DH], attended[:, DH:])
    left = jnp.concatenate([own, near[...]], axis=0).T
    half = left.shape[1] // 2
    chunk = grad.shape[1] // out.shape[0]
    wide = 4
    for s in range(0, out.shape[0], wide):
        at = slice(s * chunk, (s + wide) * chunk)
        term = jnp.dot(left[:, :half], grad[:, at], preferred_element_type=F32)
        term += jnp.dot(left[:, half:], near_grad[:, at], preferred_element_type=F32)
        term = term.astype(BF)
        for i in range(wide):
            out[s + i] = term[:, i * chunk : (i + 1) * chunk]


def partial_grad(place, attended, near, grad, near_grad, buckets):
    return pl.pallas_call(
        partial_kernel,
        out_shape=jax.ShapeDtypeStruct((buckets, DH, grad.shape[1] // buckets), BF),
        in_specs=[SMEM, VMEM, VMEM, VMEM, VMEM],
        out_specs=VMEM,
        compiler_params=params(),
    )(place, attended, near, grad, near_grad)


def total_kernel(parts, out):
    for core in range(2):
        total = parts[core].astype(F32)
        for p in range(1, parts.shape[0] // 2):
            total += parts[2 * p + core].astype(F32)
        out[core * DH : (core + 1) * DH] = total


def total_grad(parts):
    return pl.pallas_call(
        total_kernel,
        out_shape=jax.ShapeDtypeStruct((2 * DH, parts.shape[2]), F32),
        in_specs=[VMEM],
        out_specs=VMEM,
        compiler_params=params(),
    )(parts)


def shift(x, axis, step):
    n = lax.axis_size(axis)
    return lax.ppermute(x, axis, [(i, (i + step) % n) for i in range(n)])


def sibling(x):
    n = lax.axis_size("seq")
    return lax.ppermute(x, "seq", [(i, i ^ 1) for i in range(n)])


def everywhere(x, axis, groups=None):
    n = lax.axis_size(axis) if groups is None else len(groups[0])
    copies = jnp.broadcast_to(x[None], (n,) + x.shape)
    return lax.all_to_all(
        copies, axis, split_axis=0, concat_axis=0, axis_index_groups=groups, tiled=True
    )


def exchange(x):
    return lax.all_to_all(x, "seq", split_axis=0, concat_axis=0, tiled=True)


def local(
    span_states, dec_query, nbr_query, nbr_index, nbr_count, wkv_enc, wo_enc, wkv_dec, grad_out
):
    devices = lax.axis_size("seq")
    groups = lax.axis_size("mp")
    s, z = lax.axis_index("seq"), lax.axis_index("mp")
    core, chip = s % 2, s // 2
    place = jnp.stack([z, core]).astype(jnp.int32)
    spans = nbr_count.shape[0]
    rows = nbr_query.shape[0]
    hidden = span_states.shape[1]
    same_core = [[2 * p + c for p in range(devices // 2)] for c in range(2)]

    home = nbr_index // rows
    mine = jnp.arange(devices, dtype=jnp.int32)[:, None, None] == home[None]
    tags = jnp.sum(jnp.where(mine, (nbr_index % rows + 1)[None], 0), axis=(1, 2))
    tags = exchange(tags.reshape(devices, 1, 1)).reshape(devices)
    box0, box1 = outbox(tags, nbr_query, devices)
    in0 = exchange(box0)
    in1 = exchange(box1)

    part = DH // (devices // 2)
    wo_rows = lax.dynamic_slice_in_dim(wo_enc, core * DH + chip * part, part, 0)
    wo_rows = everywhere(wo_rows, "mp").reshape(groups * part, hidden)
    product = jnp.dot(
        wo_rows, wkv_dec.reshape(hidden, -1), preferred_element_type=F32
    ).astype(BF)
    product = everywhere(product, "seq", same_core)
    product = product.reshape(devices // 2, groups, part, -1).transpose(1, 0, 2, 3)
    product = product.reshape(groups, DH, -1)
    product_far = sibling(product)

    pairs = jnp.dot(
        span_states, wkv_enc.reshape(hidden, -1), preferred_element_type=F32
    ).astype(BF)
    values = everywhere(pairs[:, 2 * DH :], "mp")
    folded = fold(place, values, product, product_far, spans)
    grad_near = sibling(grad_out)

    def ring(x, forward):
        up = [x]
        down = [x]
        for _ in range(3):
            up.append(shift(up[-1], "mp", -1))
            down.append(shift(down[-1], "mp", 1))
        last = shift(up[-1], "mp", -1) if forward else shift(down[-1], "mp", 1)
        return up + [last] + down[:0:-1]

    w0 = ring(encode(0, nbr_index, in0, pairs), True)
    w1 = ring(encode(1, nbr_index, in1, pairs), False)
    pieces = [piece for both in zip(w0, w1) for piece in both]
    attended, send = decode(place, nbr_count, folded, dec_query, pieces)

    near = sibling(send)
    parts = exchange(partial_grad(place, attended, near, grad_out, grad_near, devices))
    return attended, total_grad(parts)


def solution(mesh):
    return jax.shard_map(
        local,
        mesh=mesh,
        in_specs=(
            P("seq", None),
            P("seq", "mp"),
            P("seq", None, "mp"),
            P("seq", None),
            P("seq"),
            P(None, None, "mp"),
            P("mp", None),
            P(None, None, "mp"),
            P("seq", None),
        ),
        out_specs=(P("seq", "mp"), P("mp", "seq")),
        check_vma=False,
    )
```

```python
import functools
import math

import jax
import jax.numpy as jnp
from jax import lax
from jax.experimental import pallas as pl
from jax.experimental.pallas import tpu as pltpu
from jax.sharding import Mesh, PartitionSpec as P

DH = 128
BF = jnp.bfloat16
F32 = jnp.float32
VMEM = pl.BlockSpec(memory_space=pltpu.VMEM)
SMEM = pl.BlockSpec(memory_space=pltpu.SMEM)
HBM = pl.BlockSpec(memory_space=pltpu.HBM)
SEQ = ("chip", "core")
ANY = pl.BlockSpec(memory_space=pl.ANY)
NT = (((1,), (1,)), ((), ()))


def params(mebibytes=16):
    return pltpu.CompilerParams(vmem_limit_bytes=mebibytes * 1024 * 1024)


def tags_kernel(rows, index, out):
    spans, slots = index.shape
    for dest in range(out.shape[0]):
        out[dest, 0, 0] = 0
    for j in range(spans * slots):
        entry = index[j // slots, j % slots]
        out[entry // rows, 0, 0] = entry % rows + 1


def make_tags(rows, index, devices):
    return pl.pallas_call(
        functools.partial(tags_kernel, rows),
        out_shape=jax.ShapeDtypeStruct((devices, 1, 1), jnp.int32),
        in_specs=[SMEM],
        out_specs=SMEM,
    )(index)


def product_kernel(place, matrix, *refs):
    pieces, (out, left, sems) = refs[:-3], refs[-3:]
    part = left.shape[0] // len(pieces)
    copies = [
        pltpu.make_async_copy(p, left.at[pl.ds(i * part, part)], sems.at[i])
        for i, p in enumerate(pieces)
    ]
    for copy in copies:
        copy.start()
    for copy in copies:
        copy.wait()
    first = pl.multiple_of(place[1] * 2 * DH, 2 * DH)
    right = matrix[:, pl.ds(first, 2 * DH)]
    result = jnp.dot(left[...], right, preferred_element_type=F32).astype(BF)
    for p in range(out.shape[0]):
        out[p] = result


def multiply(place, matrix, pieces, copies):
    return pl.pallas_call(
        product_kernel,
        out_shape=jax.ShapeDtypeStruct((copies, len(pieces) * pieces[0].shape[0], 2 * DH), BF),
        in_specs=[SMEM, VMEM] + [ANY] * len(pieces),
        out_specs=VMEM,
        scratch_shapes=[
            pltpu.VMEM((len(pieces) * pieces[0].shape[0], pieces[0].shape[1]), BF),
            pltpu.SemaphoreType.DMA((len(pieces),)),
        ],
        compiler_params=params(),
    )(place, matrix, *pieces)


def outbox_kernel(tags, query, out, sems):
    count = out.shape[0]

    def copy(dest):
        return pltpu.make_async_copy(query.at[tags[dest, 0, 0] - 1], out.at[dest], sems.at[dest])

    for dest in range(count):

        @pl.when(tags[dest, 0, 0] > 0)
        def _():
            copy(dest).start()

    for dest in range(count):

        @pl.when(tags[dest, 0, 0] > 0)
        def _():
            copy(dest).wait()


def outbox(tags, query, buckets):
    return pl.pallas_call(
        outbox_kernel,
        out_shape=jax.ShapeDtypeStruct((buckets,) + query.shape[1:], BF),
        in_specs=[SMEM, VMEM],
        out_specs=HBM,
        scratch_shapes=[pltpu.SemaphoreType.DMA((buckets,))],
        compiler_params=params(60),
    )(tags, query)


def encode_kernel(rows, index, inbox, pairs, out0, out1, held, sems):
    spans, slots = index.shape
    span_len = pairs.shape[0] // spans
    copies = []
    for j in range(spans * slots):
        home = index[j // slots, j % slots] // rows
        copies.append(pltpu.make_async_copy(inbox.at[home], held.at[j], sems.at[j]))
        copies[-1].start()
    for j in range(spans * slots):
        c, k = j // slots, j % slots
        copies[j].wait()
        for head, out in enumerate((out0, out1)):
            at = slice(head * DH, (head + 1) * DH)
            keys = pairs[c * span_len : (c + 1) * span_len, at]
            scores = lax.dot_general(
                keys, held[j, :, at], NT, preferred_element_type=F32
            ) / math.sqrt(DH)
            exponent = jnp.exp(scores - jnp.max(scores, axis=0, keepdims=True))
            weights = exponent / jnp.sum(exponent, axis=0, keepdims=True)
            out[c * span_len : (c + 1) * span_len, k * DH : (k + 1) * DH] = weights.astype(BF)
    tokens = pairs.shape[0]
    rows = tokens // slots
    for head, out in enumerate((out0, out1)):
        values = pairs[:, (2 + head) * DH : (3 + head) * DH]
        out[tokens:] = jnp.concatenate(
            [values[k * rows : (k + 1) * rows] for k in range(slots)], axis=1
        )


def encode(index, inbox, pairs):
    spans, slots = index.shape
    tokens = pairs.shape[0]
    shape = jax.ShapeDtypeStruct((tokens + tokens // slots, slots * inbox.shape[1]), BF)
    return pl.pallas_call(
        functools.partial(encode_kernel, spans * slots),
        out_shape=(shape, shape),
        in_specs=[SMEM, HBM, VMEM],
        out_specs=(VMEM, VMEM),
        scratch_shapes=[
            pltpu.VMEM((spans * slots,) + inbox.shape[1:], BF),
            pltpu.SemaphoreType.DMA((spans * slots,)),
        ],
        compiler_params=params(),
    )(index, inbox, pairs)


def absorb_kernel(tokens, *refs):
    weights, values = refs[-2:]
    spans = weights.shape[0]
    span_len = tokens // spans
    for i, piece in enumerate(refs[:-2]):
        for c in range(spans):
            weights[c, i * span_len : (i + 1) * span_len] = piece[
                c * span_len : (c + 1) * span_len
            ]
        values[i] = piece[tokens:]


def absorb(tokens, spans, pieces):
    total, width = pieces[0].shape
    return pl.pallas_call(
        functools.partial(absorb_kernel, tokens),
        out_shape=(
            jax.ShapeDtypeStruct((spans, len(pieces) * tokens // spans, width), BF),
            jax.ShapeDtypeStruct((len(pieces), total - tokens, width), BF),
        ),
        in_specs=[VMEM] * len(pieces),
        out_specs=(VMEM, VMEM),
        compiler_params=params(),
    )(*pieces)


def decode_kernel(part, order, place, counts, query, mine, *refs):
    out, send, folded, weights, values, held, sems = refs[-7:]
    groups = mine.shape[1] // part
    late = refs[:-10]
    spans = folded.shape[0]
    tokens = query.shape[0]
    span_len = tokens // spans
    core = place[1]
    slots = weights.shape[2] // DH
    slot_tokens = slots * DH
    copies = [
        pltpu.make_async_copy(source, target, sems.at[i])
        for i, (source, target) in enumerate(zip(refs[-10:-7], (values, held, weights)))
    ]
    for copy in copies:
        copy.start()
    copies[0].wait()

    def riding(i):
        first = values.shape[0]
        rows = values[i] if i < first else late[i - first][tokens:]
        return jnp.concatenate([rows[:, k * DH : (k + 1) * DH] for k in range(slots)], axis=0)

    for which, near in ((core, mine), (1 - core, held)):
        if near is held:
            copies[1].wait()
        for n, g in enumerate(order):
            at = slice(g * part, (g + 1) * part)
            rows = jnp.concatenate([near[p, at] for p in range(near.shape[0])], axis=0)
            low = jnp.dot(riding(2 * n), rows[:DH], preferred_element_type=F32)
            high = jnp.dot(riding(2 * n + 1), rows[DH:], preferred_element_type=F32)
            for c in range(spans):
                span = slice(c * span_len, (c + 1) * span_len)
                both = jnp.concatenate([low[span], high[span]], axis=0)
                first = pl.multiple_of(which * 2 * DH, 2 * DH)
                columns = slice(n * 2 * span_len, (n + 1) * 2 * span_len)
                folded[c, pl.ds(first, 2 * DH), columns] = both.T.astype(BF)
    copies[2].wait()
    early = weights.shape[1]
    for c in range(spans):
        rest = jnp.concatenate([p[c * span_len : (c + 1) * span_len] for p in late], axis=0)
        both = jnp.dot(folded[c, :, :early], weights[c], preferred_element_type=F32)
        both += jnp.dot(folded[c, :, early:], rest, preferred_element_type=F32)
        both = both.astype(BF)
        usable = lax.broadcasted_iota(jnp.int32, (span_len, slot_tokens), 1) < counts[c] * DH
        for h in range(2):
            at = slice(c * span_len, (c + 1) * span_len)
            keys = both[h * DH : (h + 1) * DH]
            head_values = both[(2 + h) * DH : (3 + h) * DH]
            scores = jnp.dot(
                query[at, h * DH : (h + 1) * DH], keys, preferred_element_type=F32
            ) / math.sqrt(DH)
            scores = jnp.where(usable, scores, -1e30)
            exponent = jnp.exp(scores - jnp.max(scores, axis=1, keepdims=True))
            share = (exponent / jnp.sum(exponent, axis=1, keepdims=True)).astype(BF)
            result = lax.dot_general(share, head_values, NT, preferred_element_type=F32)
            out[at, h * DH : (h + 1) * DH] = result.astype(BF)
    send[...] = jnp.where(core == 0, out[:, DH:], out[:, :DH])


def decode(place, counts, query, mine, held, values, late, other, order):
    tokens, width = query.shape
    spans = counts.shape[0]
    groups = len(order)
    part = mine.shape[1] // groups
    return pl.pallas_call(
        functools.partial(decode_kernel, part, order),
        out_shape=(
            jax.ShapeDtypeStruct((tokens, width), BF),
            jax.ShapeDtypeStruct((tokens, DH), BF),
        ),
        in_specs=[SMEM, SMEM] + [VMEM] * (2 + len(late)) + [ANY] * 3,
        out_specs=(VMEM, VMEM),
        scratch_shapes=[
            pltpu.VMEM((spans, 4 * DH, 2 * groups * tokens // spans), BF),
            pltpu.VMEM(held.shape, BF),
            pltpu.VMEM(values.shape, BF),
            pltpu.VMEM(mine.shape, BF),
            pltpu.SemaphoreType.DMA((3,)),
        ],
        compiler_params=params(),
    )(place, counts, query, mine, *late, values, other, held)


def partial_kernel(place, attended, near, grad, near_grad, out):
    own = jnp.where(place[1] == 0, attended[:, :DH], attended[:, DH:])
    left = jnp.concatenate([own, near[...]], axis=0).T
    half = left.shape[1] // 2
    chunk = grad.shape[1] // out.shape[0]
    wide = 4
    for s in range(0, out.shape[0], wide):
        at = slice(s * chunk, (s + wide) * chunk)
        term = jnp.dot(left[:, :half], grad[:, at], preferred_element_type=F32)
        term += jnp.dot(left[:, half:], near_grad[:, at], preferred_element_type=F32)
        term = term.astype(BF)
        for i in range(wide):
            out[s + i] = term[:, i * chunk : (i + 1) * chunk]


def partial_grad(place, attended, near, grad, near_grad, buckets):
    return pl.pallas_call(
        partial_kernel,
        out_shape=jax.ShapeDtypeStruct((buckets, DH, grad.shape[1] // buckets), BF),
        in_specs=[SMEM, VMEM, VMEM, VMEM, VMEM],
        out_specs=VMEM,
        compiler_params=params(),
    )(place, attended, near, grad, near_grad)


def total_kernel(parts, out):
    for core in range(2):
        total = parts[core].astype(F32)
        for p in range(1, parts.shape[0] // 2):
            total += parts[2 * p + core].astype(F32)
        out[core * DH : (core + 1) * DH] = total


def total_grad(parts):
    return pl.pallas_call(
        total_kernel,
        out_shape=jax.ShapeDtypeStruct((2 * DH, parts.shape[2]), F32),
        in_specs=[VMEM],
        out_specs=VMEM,
        compiler_params=params(),
    )(parts)


def shift(x, axis, step):
    n = lax.axis_size(axis)
    return lax.ppermute(x, axis, [(i, (i + step) % n) for i in range(n)])


def sibling(x):
    return lax.ppermute(x, "core", [(0, 1), (1, 0)])


def exchange_over(x, axis):
    return lax.all_to_all(x, axis, split_axis=0, concat_axis=0, tiled=True)


def exchange(x):
    return lax.all_to_all(x, SEQ, split_axis=0, concat_axis=0, tiled=True)


def local(
    span_states, dec_query, nbr_query, nbr_index, nbr_count, wkv_enc, wo_enc, wkv_dec, grad_out
):
    chips = lax.axis_size("chip")
    devices = 2 * chips
    groups = lax.axis_size("mp")
    chip, core, z = lax.axis_index("chip"), lax.axis_index("core"), lax.axis_index("mp")
    place = jnp.stack([z, core]).astype(jnp.int32)
    spans = nbr_count.shape[0]
    rows = nbr_query.shape[0]
    hidden = span_states.shape[1]

    def ring(x, forward):
        up = [x]
        down = [x]
        for _ in range(3):
            up.append(shift(up[-1], "mp", -1))
            down.append(shift(down[-1], "mp", 1))
        last = shift(up[-1], "mp", -1) if forward else shift(down[-1], "mp", 1)
        return up + [last] + down[:0:-1]

    tags = exchange(make_tags(rows, nbr_index, devices))

    pairs = jnp.dot(
        span_states, wkv_enc.reshape(hidden, -1), preferred_element_type=F32
    ).astype(BF)
    part = 2 * DH // chips
    wo_rows = lax.dynamic_slice_in_dim(wo_enc, chip * part, part, 0)
    tags, wo_rows, pairs = lax.optimization_barrier((tags, wo_rows, pairs))

    box = outbox(tags, nbr_query, devices)
    box, wkv_dec, wo_rows, pairs = lax.optimization_barrier((box, wkv_dec, wo_rows, pairs))
    inbox = exchange(box)

    wo_rows = ring(wo_rows, True)
    product = multiply(place, wkv_dec.reshape(hidden, -1), wo_rows, chips)
    grad_near = sibling(grad_out)
    inbox, product, grad_near = lax.optimization_barrier((inbox, product, grad_near))

    w0, w1 = encode(nbr_index, inbox, pairs)
    product = exchange_over(product, "chip")

    up, down = [[w0, w1]], [[w0, w1]]
    for _ in range(3):
        up.append([shift(w, "mp", -1) for w in up[-1]])
        down.append([shift(w, "mp", 1) for w in down[-1]])
    first = [w0, w1] + up[1] + down[1] + up[2] + down[2]
    held, values = absorb(pairs.shape[0], spans, first)
    held, values, up[3][0], down[3][1], product = lax.optimization_barrier(
        (held, values, up[3][0], down[3][1], product)
    )
    far = sibling(product)
    last = [shift(up[3][0], "mp", -1), shift(down[3][1], "mp", 1)]
    order = (0, 1, groups - 1, 2, groups - 2, 3, groups - 3, 4)
    attended, send = decode(
        place, nbr_count, dec_query, product, held, values, up[3] + down[3] + last, far, order
    )

    near = sibling(send)
    parts = exchange(partial_grad(place, attended, near, grad_out, grad_near, devices))
    return attended, total_grad(parts)


def solution(mesh):
    devices = mesh.devices
    fine = Mesh(devices.reshape(-1, 2, devices.shape[1]), SEQ + ("mp",))
    return jax.shard_map(
        local,
        mesh=fine,
        in_specs=(
            P(SEQ, None),
            P(SEQ, "mp"),
            P(SEQ, None, "mp"),
            P(SEQ, None),
            P(SEQ),
            P(None, None, "mp"),
            P("mp", None),
            P(None, None, "mp"),
            P(SEQ, None),
        ),
        out_specs=(P(SEQ, "mp"), P("mp", SEQ)),
        check_vma=False,
    )
```

```python
import functools
import math

import jax
import jax.numpy as jnp
from jax import lax
from jax.experimental import pallas as pl
from jax.experimental.pallas import tpu as pltpu
from jax.sharding import Mesh, PartitionSpec as P

DH = 128
BF = jnp.bfloat16
F32 = jnp.float32
VMEM = pl.BlockSpec(memory_space=pltpu.VMEM)
SMEM = pl.BlockSpec(memory_space=pltpu.SMEM)
HBM = pl.BlockSpec(memory_space=pltpu.HBM)
SEQ = ("chip", "core")
ANY = pl.BlockSpec(memory_space=pl.ANY)
NT = (((1,), (1,)), ((), ()))


def params(mebibytes=16):
    return pltpu.CompilerParams(vmem_limit_bytes=mebibytes * 1024 * 1024)


def tags_kernel(rows, index, out):
    spans, slots = index.shape
    for dest in range(out.shape[0]):
        out[dest, 0, 0] = 0
    for j in range(spans * slots):
        entry = index[j // slots, j % slots]
        out[entry // rows, 0, 0] = entry % rows + 1


def make_tags(rows, index, devices):
    return pl.pallas_call(
        functools.partial(tags_kernel, rows),
        out_shape=jax.ShapeDtypeStruct((devices, 1, 1), jnp.int32),
        in_specs=[SMEM],
        out_specs=SMEM,
    )(index)


def product_kernel(place, matrix, *refs):
    pieces, (out, left, result, sems) = refs[:-4], refs[-4:]
    part = left.shape[0] // len(pieces)
    copies = [
        pltpu.make_async_copy(p, left.at[pl.ds(i * part, part)], sems.at[i])
        for i, p in enumerate(pieces)
    ]
    for copy in copies:
        copy.start()
    for copy in copies:
        copy.wait()
    first = pl.multiple_of(place[1] * 2 * DH, 2 * DH)
    right = matrix[:, pl.ds(first, 2 * DH)]
    result[...] = jnp.dot(left[...], right, preferred_element_type=F32).astype(BF)
    copies = [
        pltpu.make_async_copy(result, out.at[p], sems.at[p]) for p in range(out.shape[0])
    ]
    for copy in copies:
        copy.start()
    for copy in copies:
        copy.wait()


def multiply(place, matrix, pieces, copies):
    rows = len(pieces) * pieces[0].shape[0]
    pieces = [pltpu.with_memory_space_constraint(p, pltpu.HBM) for p in pieces]
    return pl.pallas_call(
        product_kernel,
        out_shape=pltpu.HBM((copies, rows, 2 * DH), BF),
        in_specs=[SMEM, VMEM] + [HBM] * len(pieces),
        out_specs=HBM,
        scratch_shapes=[
            pltpu.VMEM((rows, pieces[0].shape[1]), BF),
            pltpu.VMEM((rows, 2 * DH), BF),
            pltpu.SemaphoreType.DMA((max(copies, len(pieces)),)),
        ],
        compiler_params=params(),
    )(place, matrix, *pieces)


def outbox_kernel(tags, query, out, sems):
    count = out.shape[0]

    def copy(dest):
        return pltpu.make_async_copy(query.at[tags[dest, 0, 0] - 1], out.at[dest], sems.at[dest])

    for dest in range(count):

        @pl.when(tags[dest, 0, 0] > 0)
        def _():
            copy(dest).start()

    for dest in range(count):

        @pl.when(tags[dest, 0, 0] > 0)
        def _():
            copy(dest).wait()


def outbox(tags, query, buckets):
    return pl.pallas_call(
        outbox_kernel,
        out_shape=jax.ShapeDtypeStruct((buckets,) + query.shape[1:], BF),
        in_specs=[SMEM, VMEM],
        out_specs=HBM,
        scratch_shapes=[pltpu.SemaphoreType.DMA((buckets,))],
        compiler_params=params(60),
    )(tags, query)


def encode_kernel(rows, index, inbox, pairs, out0, out1, held, sems):
    spans, slots = index.shape
    span_len = pairs.shape[0] // spans
    copies = []
    for j in range(spans * slots):
        home = index[j // slots, j % slots] // rows
        copies.append(pltpu.make_async_copy(inbox.at[home], held.at[j], sems.at[j]))
        copies[-1].start()
    for c in range(spans):
        for j in range(c * slots, (c + 1) * slots):
            copies[j].wait()
        for head, out in enumerate((out0, out1)):
            at = slice(head * DH, (head + 1) * DH)
            keys = pairs[c * span_len : (c + 1) * span_len, at]
            queries = held[c * slots : (c + 1) * slots, :, at].reshape(-1, DH)
            scores = lax.dot_general(
                keys, queries, NT, preferred_element_type=F32
            ) / math.sqrt(DH)
            exponent = jnp.exp(scores - jnp.max(scores, axis=0, keepdims=True))
            weights = exponent / jnp.sum(exponent, axis=0, keepdims=True)
            out[c * span_len : (c + 1) * span_len] = weights.astype(BF)
    tokens = pairs.shape[0]
    rows = tokens // slots
    for head, out in enumerate((out0, out1)):
        values = pairs[:, (2 + head) * DH : (3 + head) * DH]
        out[tokens:] = jnp.concatenate(
            [values[k * rows : (k + 1) * rows] for k in range(slots)], axis=1
        )


def encode(index, inbox, pairs):
    spans, slots = index.shape
    tokens = pairs.shape[0]
    shape = jax.ShapeDtypeStruct((tokens + tokens // slots, slots * inbox.shape[1]), BF)
    return pl.pallas_call(
        functools.partial(encode_kernel, spans * slots),
        out_shape=(shape, shape),
        in_specs=[SMEM, HBM, VMEM],
        out_specs=(VMEM, VMEM),
        scratch_shapes=[
            pltpu.VMEM((spans * slots,) + inbox.shape[1:], BF),
            pltpu.SemaphoreType.DMA((spans * slots,)),
        ],
        compiler_params=params(),
    )(index, inbox, pairs)


def decode_kernel(part, order, place, counts, query, product, *refs):
    out, send, folded, held, pieces, sems = refs[-6:]
    groups = len(order)
    spans = folded.shape[0]
    tokens = query.shape[0]
    span_len = tokens // spans
    slots = pieces.shape[2] // DH
    slot_tokens = slots * DH
    copies = [
        pltpu.make_async_copy(product.at[:, k], held.at[k], sems.at[k]) for k in range(2)
    ]
    arrive = [
        pltpu.make_async_copy(piece, pieces.at[i], sems.at[2 + i])
        for i, piece in enumerate(refs[:-6])
    ]
    for copy in copies[:1] + arrive + copies[1:]:
        copy.start()

    def riding(i):
        rows = pieces[i][tokens:]
        return jnp.concatenate([rows[:, k * DH : (k + 1) * DH] for k in range(slots)], axis=0)

    for k in range(2):
        copies[k].wait()
        for n, g in enumerate(order):
            if k == 0:
                arrive[2 * n].wait()
                arrive[2 * n + 1].wait()
            at = slice(g * part, (g + 1) * part)
            rows = jnp.concatenate([held[k, p, at] for p in range(held.shape[1])], axis=0)
            low = jnp.dot(riding(2 * n), rows[:DH], preferred_element_type=F32)
            high = jnp.dot(riding(2 * n + 1), rows[DH:], preferred_element_type=F32)
            for c in range(spans):
                span = slice(c * span_len, (c + 1) * span_len)
                both = jnp.concatenate([low[span], high[span]], axis=0).astype(BF)
                columns = slice(n * 2 * span_len, (n + 1) * 2 * span_len)
                folded[c, k * 2 * DH : (k + 1) * 2 * DH, columns] = both.T
    for c in range(spans):
        weights = pieces[:, c * span_len : (c + 1) * span_len].reshape(-1, slot_tokens)
        both = jnp.dot(folded[c], weights, preferred_element_type=F32).astype(BF)
        usable = lax.broadcasted_iota(jnp.int32, (span_len, slot_tokens), 1) < counts[c] * DH
        for h in range(2):
            at = slice(c * span_len, (c + 1) * span_len)
            keys = both[h * DH : (h + 1) * DH]
            head_values = both[(2 + h) * DH : (3 + h) * DH]
            scores = jnp.dot(
                query[at, h * DH : (h + 1) * DH], keys, preferred_element_type=F32
            ) / math.sqrt(DH)
            scores = jnp.where(usable, scores, -1e30)
            exponent = jnp.exp(scores - jnp.max(scores, axis=1, keepdims=True))
            share = (exponent / jnp.sum(exponent, axis=1, keepdims=True)).astype(BF)
            result = lax.dot_general(share, head_values, NT, preferred_element_type=F32)
            out[at, h * DH : (h + 1) * DH] = result.astype(BF)
    send[...] = out[...]


def decode(place, counts, query, product, pieces, order):
    tokens, width = query.shape
    spans = counts.shape[0]
    part = product.shape[2] // len(order)
    shape = jax.ShapeDtypeStruct((tokens, width), BF)
    return pl.pallas_call(
        functools.partial(decode_kernel, part, order),
        out_shape=(shape, shape),
        in_specs=[SMEM, SMEM, VMEM, ANY] + [HBM] * len(pieces),
        out_specs=(VMEM, VMEM),
        scratch_shapes=[
            pltpu.VMEM((spans, 4 * DH, 2 * len(order) * tokens // spans), BF),
            pltpu.VMEM((2, product.shape[0]) + product.shape[2:], BF),
            pltpu.VMEM((len(pieces),) + pieces[0].shape, BF),
            pltpu.SemaphoreType.DMA((2 + len(pieces),)),
        ],
        compiler_params=params(),
    )(place, counts, query, product, *pieces)


def partial_kernel(place, attended, near, grad, near_grad, out):
    left = jnp.concatenate([attended[...], near[...]], axis=0).T
    width = out.shape[2]

    def block(p):
        at = pl.ds(pl.multiple_of((2 * p + place[1]) * width, width), width)
        return jnp.concatenate([grad[:, at], near_grad[:, at]], axis=0)

    for p in range(0, out.shape[0], 2):
        right = jnp.concatenate([block(p), block(p + 1)], axis=1)
        term = jnp.dot(left, right, preferred_element_type=F32).astype(BF)
        out[p] = term[:, :width]
        out[p + 1] = term[:, width:]


def partial_grad(place, attended, near, grad, near_grad, chips):
    return pl.pallas_call(
        partial_kernel,
        out_shape=jax.ShapeDtypeStruct(
            (chips, attended.shape[1], grad.shape[1] // (2 * chips)), BF
        ),
        in_specs=[SMEM, VMEM, VMEM, VMEM, VMEM],
        out_specs=VMEM,
        compiler_params=params(),
    )(place, attended, near, grad, near_grad)


def total_kernel(parts, out):
    total = parts[0].astype(F32)
    for p in range(1, parts.shape[0]):
        total += parts[p].astype(F32)
    out[...] = total


def total_grad(parts):
    return pl.pallas_call(
        total_kernel,
        out_shape=jax.ShapeDtypeStruct(parts.shape[1:], F32),
        in_specs=[VMEM],
        out_specs=VMEM,
        compiler_params=params(),
    )(parts)


def shift(x, axis, step):
    n = lax.axis_size(axis)
    return lax.ppermute(x, axis, [(i, (i + step) % n) for i in range(n)])


def sibling(x):
    return lax.ppermute(x, "core", [(0, 1), (1, 0)])


def exchange_over(x, axis):
    return lax.all_to_all(x, axis, split_axis=0, concat_axis=0, tiled=True)


def exchange(x):
    return lax.all_to_all(x, SEQ, split_axis=0, concat_axis=0, tiled=True)


def local(
    span_states, dec_query, nbr_query, nbr_index, nbr_count, wkv_enc, wo_enc, wkv_dec, grad_out
):
    chips = lax.axis_size("chip")
    devices = 2 * chips
    groups = lax.axis_size("mp")
    chip, core, z = lax.axis_index("chip"), lax.axis_index("core"), lax.axis_index("mp")
    place = jnp.stack([z, core]).astype(jnp.int32)
    spans = nbr_count.shape[0]
    rows = nbr_query.shape[0]
    hidden = span_states.shape[1]

    def ring(x, forward):
        up = [x]
        down = [x]
        for _ in range(3):
            up.append(shift(up[-1], "mp", -1))
            down.append(shift(down[-1], "mp", 1))
        last = shift(up[-1], "mp", -1) if forward else shift(down[-1], "mp", 1)
        return up + [last] + down[:0:-1]

    tags = exchange(make_tags(rows, nbr_index, devices))

    pairs = jnp.dot(
        span_states, wkv_enc.reshape(hidden, -1), preferred_element_type=F32
    ).astype(BF)
    part = 2 * DH // chips
    wo_rows = lax.dynamic_slice_in_dim(wo_enc, chip * part, part, 0)
    tags, wo_rows, pairs = lax.optimization_barrier((tags, wo_rows, pairs))

    box = outbox(tags, nbr_query, devices)
    box, wkv_dec, wo_rows, pairs = lax.optimization_barrier((box, wkv_dec, wo_rows, pairs))
    inbox = exchange(box)

    wo_rows = ring(wo_rows, True)
    product = multiply(place, wkv_dec.reshape(hidden, -1), wo_rows, devices)
    grad_near = sibling(grad_out)
    inbox, product, grad_near = lax.optimization_barrier((inbox, product, grad_near))

    w0, w1 = encode(nbr_index, inbox, pairs)
    product = exchange(product).reshape((chips, 2) + product.shape[1:])

    up, down = [[w0, w1]], [[w0, w1]]
    for _ in range(3):
        up.append([shift(w, "mp", -1) for w in up[-1]])
        down.append([shift(w, "mp", 1) for w in down[-1]])
    last = [shift(up[3][0], "mp", -1), shift(down[3][1], "mp", 1)]
    pieces = [w0, w1] + [w for step in zip(up[1:], down[1:]) for side in step for w in side]
    order = (0, 1, groups - 1, 2, groups - 2, 3, groups - 3, 4)
    pieces = [pltpu.with_memory_space_constraint(w, pltpu.HBM) for w in pieces + last]
    attended, send = decode(place, nbr_count, dec_query, product, pieces, order)

    near = sibling(send)
    parts = partial_grad(place, send, near, grad_out, grad_near, chips)
    parts = exchange_over(parts, "chip")
    return attended, total_grad(parts)


def solution(mesh):
    devices = mesh.devices
    fine = Mesh(devices.reshape(-1, 2, devices.shape[1]), SEQ + ("mp",))
    return jax.shard_map(
        local,
        mesh=fine,
        in_specs=(
            P(SEQ, None),
            P(SEQ, "mp"),
            P(SEQ, None, "mp"),
            P(SEQ, None),
            P(SEQ),
            P(None, None, "mp"),
            P("mp", None),
            P(None, None, "mp"),
            P(SEQ, None),
        ),
        out_specs=(P(SEQ, "mp"), P("mp", SEQ)),
        check_vma=False,
    )
```

```python
import functools
import math

import jax
import jax.numpy as jnp
from jax import lax
from jax.experimental import pallas as pl
from jax.experimental.pallas import tpu as pltpu
from jax.sharding import Mesh, PartitionSpec as P

DH = 128
BF = jnp.bfloat16
F32 = jnp.float32
VMEM = pl.BlockSpec(memory_space=pltpu.VMEM)
SMEM = pl.BlockSpec(memory_space=pltpu.SMEM)
HBM = pl.BlockSpec(memory_space=pltpu.HBM)
SEQ = ("chip", "core")
ANY = pl.BlockSpec(memory_space=pl.ANY)
NT = (((1,), (1,)), ((), ()))


def params(mebibytes=16):
    return pltpu.CompilerParams(vmem_limit_bytes=mebibytes * 1024 * 1024)


def tags_kernel(rows, index, out):
    spans, slots = index.shape
    for dest in range(out.shape[0]):
        out[dest, 0, 0] = 0
    for j in range(spans * slots):
        entry = index[j // slots, j % slots]
        out[entry // rows, 0, 0] = entry % rows + 1


def make_tags(rows, index, devices):
    return pl.pallas_call(
        functools.partial(tags_kernel, rows),
        out_shape=jax.ShapeDtypeStruct((devices, 1, 1), jnp.int32),
        in_specs=[SMEM],
        out_specs=SMEM,
    )(index)


def product_kernel(place, matrix, *refs):
    pieces, (out, left, result, sems) = refs[:-4], refs[-4:]
    part = left.shape[0] // len(pieces)
    copies = [
        pltpu.make_async_copy(p, left.at[pl.ds(i * part, part)], sems.at[i])
        for i, p in enumerate(pieces)
    ]
    for copy in copies:
        copy.start()
    for copy in copies:
        copy.wait()
    first = pl.multiple_of(place[1] * 2 * DH, 2 * DH)
    right = matrix[:, pl.ds(first, 2 * DH)]
    result[...] = jnp.dot(left[...], right, preferred_element_type=F32).astype(BF)
    copies = [
        pltpu.make_async_copy(result, out.at[p], sems.at[p]) for p in range(out.shape[0])
    ]
    for copy in copies:
        copy.start()
    for copy in copies:
        copy.wait()


def multiply(place, matrix, pieces, copies):
    rows = len(pieces) * pieces[0].shape[0]
    pieces = [pltpu.with_memory_space_constraint(p, pltpu.HBM) for p in pieces]
    return pl.pallas_call(
        product_kernel,
        out_shape=pltpu.HBM((copies, rows, 2 * DH), BF),
        in_specs=[SMEM, VMEM] + [HBM] * len(pieces),
        out_specs=HBM,
        scratch_shapes=[
            pltpu.VMEM((rows, pieces[0].shape[1]), BF),
            pltpu.VMEM((rows, 2 * DH), BF),
            pltpu.SemaphoreType.DMA((max(copies, len(pieces)),)),
        ],
        compiler_params=params(),
    )(place, matrix, *pieces)


def outbox_kernel(tags, query, out, sems):
    count = out.shape[0]

    def copy(dest):
        return pltpu.make_async_copy(query.at[tags[dest, 0, 0] - 1], out.at[dest], sems.at[dest])

    for dest in range(count):

        @pl.when(tags[dest, 0, 0] > 0)
        def _():
            copy(dest).start()

    for dest in range(count):

        @pl.when(tags[dest, 0, 0] > 0)
        def _():
            copy(dest).wait()


def outbox(tags, query, buckets):
    return pl.pallas_call(
        outbox_kernel,
        out_shape=jax.ShapeDtypeStruct((buckets,) + query.shape[1:], BF),
        in_specs=[SMEM, VMEM],
        out_specs=HBM,
        scratch_shapes=[pltpu.SemaphoreType.DMA((buckets,))],
        compiler_params=params(60),
    )(tags, query)


def encode_kernel(rows, index, inbox, pairs, out0, out1, held, sems):
    spans, slots = index.shape
    span_len = pairs.shape[0] // spans
    copies = []
    for j in range(spans * slots):
        home = index[j // slots, j % slots] // rows
        copies.append(pltpu.make_async_copy(inbox.at[home], held.at[j], sems.at[j]))
        copies[-1].start()
    for c in range(spans):
        for j in range(c * slots, (c + 1) * slots):
            copies[j].wait()
        for head, out in enumerate((out0, out1)):
            at = slice(head * DH, (head + 1) * DH)
            keys = pairs[c * span_len : (c + 1) * span_len, at]
            queries = held[c * slots : (c + 1) * slots, :, at].reshape(-1, DH)
            scores = lax.dot_general(
                keys, queries, NT, preferred_element_type=F32
            ) / math.sqrt(DH)
            exponent = jnp.exp(scores - jnp.max(scores, axis=0, keepdims=True))
            weights = exponent / jnp.sum(exponent, axis=0, keepdims=True)
            out[c * span_len : (c + 1) * span_len] = weights.astype(BF)
    tokens = pairs.shape[0]
    rows = tokens // slots
    for head, out in enumerate((out0, out1)):
        values = pairs[:, (2 + head) * DH : (3 + head) * DH]
        out[tokens:] = jnp.concatenate(
            [values[k * rows : (k + 1) * rows] for k in range(slots)], axis=1
        )


def encode(index, inbox, pairs):
    spans, slots = index.shape
    tokens = pairs.shape[0]
    shape = jax.ShapeDtypeStruct((tokens + tokens // slots, slots * inbox.shape[1]), BF)
    return pl.pallas_call(
        functools.partial(encode_kernel, spans * slots),
        out_shape=(shape, shape),
        in_specs=[SMEM, HBM, VMEM],
        out_specs=(VMEM, VMEM),
        scratch_shapes=[
            pltpu.VMEM((spans * slots,) + inbox.shape[1:], BF),
            pltpu.SemaphoreType.DMA((spans * slots,)),
        ],
        compiler_params=params(),
    )(index, inbox, pairs)


def decode_kernel(part, order, place, counts, query, product, *refs):
    out, send, folded, held, pieces, sems = refs[-6:]
    groups = len(order)
    spans = folded.shape[0]
    tokens = query.shape[0]
    span_len = tokens // spans
    slots = pieces.shape[2] // DH
    slot_tokens = slots * DH
    copies = [
        pltpu.make_async_copy(product.at[:, k], held.at[k], sems.at[k]) for k in range(2)
    ]
    arrive = [
        pltpu.make_async_copy(piece, pieces.at[i], sems.at[2 + i])
        for i, piece in enumerate(refs[:-6])
    ]
    for copy in copies[:1] + arrive + copies[1:]:
        copy.start()

    def riding(i):
        rows = pieces[i][tokens:]
        return jnp.concatenate([rows[:, k * DH : (k + 1) * DH] for k in range(slots)], axis=0)

    for k in range(2):
        copies[k].wait()
        for n, g in enumerate(order):
            if k == 0:
                arrive[2 * n].wait()
                arrive[2 * n + 1].wait()
            at = slice(g * part, (g + 1) * part)
            rows = jnp.concatenate([held[k, p, at] for p in range(held.shape[1])], axis=0)
            low = jnp.dot(riding(2 * n), rows[:DH], preferred_element_type=F32)
            high = jnp.dot(riding(2 * n + 1), rows[DH:], preferred_element_type=F32)
            for c in range(spans):
                span = slice(c * span_len, (c + 1) * span_len)
                both = jnp.concatenate([low[span], high[span]], axis=0).astype(BF)
                columns = slice(n * 2 * span_len, (n + 1) * 2 * span_len)
                folded[c, k * 2 * DH : (k + 1) * 2 * DH, columns] = both.T
    for c in range(spans):
        weights = pieces[:, c * span_len : (c + 1) * span_len].reshape(-1, slot_tokens)
        both = jnp.dot(folded[c], weights, preferred_element_type=F32).astype(BF)
        usable = lax.broadcasted_iota(jnp.int32, (span_len, slot_tokens), 1) < counts[c] * DH
        for h in range(2):
            at = slice(c * span_len, (c + 1) * span_len)
            keys = both[h * DH : (h + 1) * DH]
            head_values = both[(2 + h) * DH : (3 + h) * DH]
            scores = jnp.dot(
                query[at, h * DH : (h + 1) * DH], keys, preferred_element_type=F32
            ) / math.sqrt(DH)
            scores = jnp.where(usable, scores, -1e30)
            exponent = jnp.exp(scores - jnp.max(scores, axis=1, keepdims=True))
            share = (exponent / jnp.sum(exponent, axis=1, keepdims=True)).astype(BF)
            result = lax.dot_general(share, head_values, NT, preferred_element_type=F32)
            out[at, h * DH : (h + 1) * DH] = result.astype(BF)
    send[...] = out[...]


def decode(place, counts, query, product, pieces, order):
    tokens, width = query.shape
    spans = counts.shape[0]
    part = product.shape[2] // len(order)
    shape = jax.ShapeDtypeStruct((tokens, width), BF)
    return pl.pallas_call(
        functools.partial(decode_kernel, part, order),
        out_shape=(shape, shape),
        in_specs=[SMEM, SMEM, VMEM, ANY] + [HBM] * len(pieces),
        out_specs=(VMEM, VMEM),
        scratch_shapes=[
            pltpu.VMEM((spans, 4 * DH, 2 * len(order) * tokens // spans), BF),
            pltpu.VMEM((2, product.shape[0]) + product.shape[2:], BF),
            pltpu.VMEM((len(pieces),) + pieces[0].shape, BF),
            pltpu.SemaphoreType.DMA((2 + len(pieces),)),
        ],
        compiler_params=params(),
    )(place, counts, query, product, *pieces)


def partial_kernel(place, attended, near, grad, near_grad, out):
    left = jnp.concatenate([attended[...], near[...]], axis=0).T
    width = out.shape[2]

    def block(p):
        at = pl.ds(pl.multiple_of((2 * p + place[1]) * width, width), width)
        return jnp.concatenate([grad[:, at], near_grad[:, at]], axis=0)

    for p in range(0, out.shape[0], 2):
        right = jnp.concatenate([block(p), block(p + 1)], axis=1)
        term = jnp.dot(left, right, preferred_element_type=F32).astype(BF)
        out[p] = term[:, :width]
        out[p + 1] = term[:, width:]


def partial_grad(place, attended, near, grad, near_grad, chips):
    return pl.pallas_call(
        partial_kernel,
        out_shape=jax.ShapeDtypeStruct(
            (chips, attended.shape[1], grad.shape[1] // (2 * chips)), BF
        ),
        in_specs=[SMEM, VMEM, VMEM, VMEM, VMEM],
        out_specs=VMEM,
        compiler_params=params(),
    )(place, attended, near, grad, near_grad)


def total_kernel(parts, out):
    total = parts[0].astype(F32)
    for p in range(1, parts.shape[0]):
        total += parts[p].astype(F32)
    out[...] = total


def total_grad(parts):
    return pl.pallas_call(
        total_kernel,
        out_shape=jax.ShapeDtypeStruct(parts.shape[1:], F32),
        in_specs=[VMEM],
        out_specs=VMEM,
        compiler_params=params(),
    )(parts)


def shift(x, axis, step):
    n = lax.axis_size(axis)
    return lax.ppermute(x, axis, [(i, (i + step) % n) for i in range(n)])


def sibling(x):
    return lax.ppermute(x, "core", [(0, 1), (1, 0)])


def exchange_over(x, axis):
    return lax.all_to_all(x, axis, split_axis=0, concat_axis=0, tiled=True)


def exchange(x):
    return lax.all_to_all(x, SEQ, split_axis=0, concat_axis=0, tiled=True)


def local(
    span_states, dec_query, nbr_query, nbr_index, nbr_count, wkv_enc, wo_enc, wkv_dec, grad_out
):
    chips = lax.axis_size("chip")
    devices = 2 * chips
    groups = lax.axis_size("mp")
    chip, core, z = lax.axis_index("chip"), lax.axis_index("core"), lax.axis_index("mp")
    place = jnp.stack([z, core]).astype(jnp.int32)
    spans = nbr_count.shape[0]
    rows = nbr_query.shape[0]
    hidden = span_states.shape[1]

    def ring(x, forward):
        up = [x]
        down = [x]
        for _ in range(3):
            up.append(shift(up[-1], "mp", -1))
            down.append(shift(down[-1], "mp", 1))
        last = shift(up[-1], "mp", -1) if forward else shift(down[-1], "mp", 1)
        return up + [last] + down[:0:-1]

    tags = exchange(make_tags(rows, nbr_index, devices))

    part = 2 * DH // chips
    wo_rows = lax.dynamic_slice_in_dim(wo_enc, chip * part, part, 0)
    tags, wo_rows = lax.optimization_barrier((tags, wo_rows))

    box = outbox(tags, nbr_query, devices)
    box, wkv_dec, wo_rows, wkv_enc = lax.optimization_barrier((box, wkv_dec, wo_rows, wkv_enc))
    inbox = exchange(box)

    pairs = jnp.dot(
        span_states, wkv_enc.reshape(hidden, -1), preferred_element_type=F32
    ).astype(BF)
    wo_rows = ring(wo_rows, True)
    product = multiply(place, wkv_dec.reshape(hidden, -1), wo_rows, devices)
    grad_near = sibling(grad_out)
    inbox, product, grad_near, pairs = lax.optimization_barrier(
        (inbox, product, grad_near, pairs)
    )

    w0, w1 = encode(nbr_index, inbox, pairs)
    product = exchange(product).reshape((chips, 2) + product.shape[1:])

    up, down = [[w0, w1]], [[w0, w1]]
    for _ in range(3):
        up.append([shift(w, "mp", -1) for w in up[-1]])
        down.append([shift(w, "mp", 1) for w in down[-1]])
    last = [shift(up[3][0], "mp", -1), shift(down[3][1], "mp", 1)]
    pieces = [w0, w1] + [w for step in zip(up[1:], down[1:]) for side in step for w in side]
    order = (0, 1, groups - 1, 2, groups - 2, 3, groups - 3, 4)
    pieces = [pltpu.with_memory_space_constraint(w, pltpu.HBM) for w in pieces + last]
    attended, send = decode(place, nbr_count, dec_query, product, pieces, order)

    near = sibling(send)
    parts = partial_grad(place, send, near, grad_out, grad_near, chips)
    parts = exchange_over(parts, "chip")
    return attended, total_grad(parts)


def solution(mesh):
    devices = mesh.devices
    fine = Mesh(devices.reshape(-1, 2, devices.shape[1]), SEQ + ("mp",))
    return jax.shard_map(
        local,
        mesh=fine,
        in_specs=(
            P(SEQ, None),
            P(SEQ, "mp"),
            P(SEQ, None, "mp"),
            P(SEQ, None),
            P(SEQ),
            P(None, None, "mp"),
            P("mp", None),
            P(None, None, "mp"),
            P(SEQ, None),
        ),
        out_specs=(P(SEQ, "mp"), P("mp", SEQ)),
        check_vma=False,
    )
```

```python
import functools
import math

import jax
import jax.numpy as jnp
from jax import lax
from jax.experimental import pallas as pl
from jax.experimental.pallas import tpu as pltpu
from jax.sharding import Mesh, PartitionSpec as P

DH = 128
BF = jnp.bfloat16
F32 = jnp.float32
VMEM = pl.BlockSpec(memory_space=pltpu.VMEM)
SMEM = pl.BlockSpec(memory_space=pltpu.SMEM)
HBM = pl.BlockSpec(memory_space=pltpu.HBM)
SEQ = ("chip", "core")
ANY = pl.BlockSpec(memory_space=pl.ANY)
NT = (((1,), (1,)), ((), ()))


def params(mebibytes=16):
    return pltpu.CompilerParams(vmem_limit_bytes=mebibytes * 1024 * 1024)


def tags_kernel(rows, index, out):
    spans, slots = index.shape
    for dest in range(out.shape[0]):
        out[dest, 0, 0] = 0
    for j in range(spans * slots):
        entry = index[j // slots, j % slots]
        out[entry // rows, 0, 0] = entry % rows + 1


def make_tags(rows, index, devices):
    return pl.pallas_call(
        functools.partial(tags_kernel, rows),
        out_shape=jax.ShapeDtypeStruct((devices, 1, 1), jnp.int32),
        in_specs=[SMEM],
        out_specs=SMEM,
    )(index)


def product_kernel(place, matrix, *refs):
    pieces, (out, left, result, sems) = refs[:-4], refs[-4:]
    part = left.shape[0] // len(pieces)
    copies = [
        pltpu.make_async_copy(p, left.at[pl.ds(i * part, part)], sems.at[i])
        for i, p in enumerate(pieces)
    ]
    for copy in copies:
        copy.start()
    for copy in copies:
        copy.wait()
    first = pl.multiple_of(place[1] * 2 * DH, 2 * DH)
    right = matrix[:, pl.ds(first, 2 * DH)]
    result[...] = jnp.dot(left[...], right, preferred_element_type=F32).astype(BF)
    copies = [
        pltpu.make_async_copy(result, out.at[p], sems.at[p]) for p in range(out.shape[0])
    ]
    for copy in copies:
        copy.start()
    for copy in copies:
        copy.wait()


def multiply(place, matrix, pieces, copies):
    rows = len(pieces) * pieces[0].shape[0]
    pieces = [pltpu.with_memory_space_constraint(p, pltpu.HBM) for p in pieces]
    return pl.pallas_call(
        product_kernel,
        out_shape=pltpu.HBM((copies, rows, 2 * DH), BF),
        in_specs=[SMEM, VMEM] + [HBM] * len(pieces),
        out_specs=HBM,
        scratch_shapes=[
            pltpu.VMEM((rows, pieces[0].shape[1]), BF),
            pltpu.VMEM((rows, 2 * DH), BF),
            pltpu.SemaphoreType.DMA((max(copies, len(pieces)),)),
        ],
        compiler_params=params(),
    )(place, matrix, *pieces)


def outbox_kernel(tags, query, out, sems):
    count = out.shape[0]

    def copy(dest):
        return pltpu.make_async_copy(query.at[tags[dest, 0, 0] - 1], out.at[dest], sems.at[dest])

    for dest in range(count):

        @pl.when(tags[dest, 0, 0] > 0)
        def _():
            copy(dest).start()

    for dest in range(count):

        @pl.when(tags[dest, 0, 0] > 0)
        def _():
            copy(dest).wait()


def outbox(tags, query, buckets):
    return pl.pallas_call(
        outbox_kernel,
        out_shape=jax.ShapeDtypeStruct((buckets,) + query.shape[1:], BF),
        in_specs=[SMEM, VMEM],
        out_specs=HBM,
        scratch_shapes=[pltpu.SemaphoreType.DMA((buckets,))],
        compiler_params=params(60),
    )(tags, query)


def encode_kernel(rows, index, inbox, pairs, out0, out1, held, sems):
    spans, slots = index.shape
    span_len = pairs.shape[0] // spans
    copies = []
    for j in range(spans * slots):
        home = index[j // slots, j % slots] // rows
        copies.append(pltpu.make_async_copy(inbox.at[home], held.at[j], sems.at[j]))
        copies[-1].start()
    for c in range(spans):
        for j in range(c * slots, (c + 1) * slots):
            copies[j].wait()
        for head, out in enumerate((out0, out1)):
            at = slice(head * DH, (head + 1) * DH)
            keys = pairs[c * span_len : (c + 1) * span_len, at]
            queries = held[c * slots : (c + 1) * slots, :, at].reshape(-1, DH)
            scores = lax.dot_general(
                keys, queries, NT, preferred_element_type=F32
            ) / math.sqrt(DH)
            exponent = jnp.exp(scores - jnp.max(scores, axis=0, keepdims=True))
            weights = exponent / jnp.sum(exponent, axis=0, keepdims=True)
            out[c * span_len : (c + 1) * span_len] = weights.astype(BF)
    tokens = pairs.shape[0]
    rows = tokens // slots
    for head, out in enumerate((out0, out1)):
        values = pairs[:, (2 + head) * DH : (3 + head) * DH]
        out[tokens:] = jnp.concatenate(
            [values[k * rows : (k + 1) * rows] for k in range(slots)], axis=1
        )


def encode(index, inbox, pairs):
    spans, slots = index.shape
    tokens = pairs.shape[0]
    shape = jax.ShapeDtypeStruct((tokens + tokens // slots, slots * inbox.shape[1]), BF)
    return pl.pallas_call(
        functools.partial(encode_kernel, spans * slots),
        out_shape=(shape, shape),
        in_specs=[SMEM, HBM, VMEM],
        out_specs=(VMEM, VMEM),
        scratch_shapes=[
            pltpu.VMEM((spans * slots,) + inbox.shape[1:], BF),
            pltpu.SemaphoreType.DMA((spans * slots,)),
        ],
        compiler_params=params(),
    )(index, inbox, pairs)


def project(part, order, ranges, product, sources, folded, held, pieces, sems):
    spans = folded.shape[0]
    span_len = folded.shape[2] // (2 * len(order))
    tokens = spans * span_len
    slots = pieces.shape[2] // DH
    arrive = [
        pltpu.make_async_copy(piece, pieces.at[i], sems.at[i])
        for i, piece in enumerate(sources)
    ]
    copies = []
    for k in range(2):
        for first, last in ranges:
            rows = pl.ds(first * part, (last - first) * part)
            copies.append(
                pltpu.make_async_copy(
                    product.at[:, k, rows],
                    held.at[k, :, rows],
                    sems.at[len(arrive) + len(copies)],
                )
            )
    each = len(ranges)
    for copy in copies[:each] + arrive + copies[each:]:
        copy.start()

    def riding(i):
        rows = pieces[i][tokens:]
        return jnp.concatenate([rows[:, k * DH : (k + 1) * DH] for k in range(slots)], axis=0)

    for k in range(2):
        for copy in copies[k * each : (k + 1) * each]:
            copy.wait()
        for n, g in enumerate(order):
            if k == 0:
                arrive[2 * n].wait()
                arrive[2 * n + 1].wait()
            at = slice(g * part, (g + 1) * part)
            rows = jnp.concatenate([held[k, p, at] for p in range(held.shape[1])], axis=0)
            low = jnp.dot(riding(2 * n), rows[:DH], preferred_element_type=F32)
            high = jnp.dot(riding(2 * n + 1), rows[DH:], preferred_element_type=F32)
            for c in range(spans):
                span = slice(c * span_len, (c + 1) * span_len)
                both = jnp.concatenate([low[span], high[span]], axis=0).astype(BF)
                columns = slice(n * 2 * span_len, (n + 1) * 2 * span_len)
                folded[c, k * 2 * DH : (k + 1) * 2 * DH, columns] = both.T
    result = []
    for c in range(spans):
        weights = pieces[:, c * span_len : (c + 1) * span_len].reshape(-1, slots * DH)
        result.append(jnp.dot(folded[c], weights, preferred_element_type=F32))
    return result


def scratch(spans, tokens, order, ranges, product, pieces):
    return [
        pltpu.VMEM((spans, 4 * DH, 2 * len(order) * tokens // spans), BF),
        pltpu.VMEM((2, product.shape[0]) + product.shape[2:], BF),
        pltpu.VMEM((len(pieces),) + pieces[0].shape, BF),
        pltpu.SemaphoreType.DMA((len(pieces) + 2 * len(ranges),)),
    ]


def begin_kernel(part, order, ranges, product, *refs):
    out, folded, held, pieces, sems = refs[-5:]
    for c, both in enumerate(
        project(part, order, ranges, product, refs[:-5], folded, held, pieces, sems)
    ):
        out[c] = both


def begin(spans, tokens, part, order, ranges, product, pieces):
    pieces = [pltpu.with_memory_space_constraint(w, pltpu.HBM) for w in pieces]
    return pl.pallas_call(
        functools.partial(begin_kernel, part, order, ranges),
        out_shape=jax.ShapeDtypeStruct((spans, 4 * DH, pieces[0].shape[1]), F32),
        in_specs=[HBM] * (1 + len(pieces)),
        out_specs=VMEM,
        scratch_shapes=scratch(spans, tokens, order, ranges, product, pieces),
        compiler_params=params(),
    )(product, *pieces)


def decode_kernel(part, order, ranges, counts, query, early, product, *refs):
    out, send, folded, held, pieces, sems = refs[-6:]
    spans = folded.shape[0]
    span_len = query.shape[0] // spans
    late = project(part, order, ranges, product, refs[:-6], folded, held, pieces, sems)
    for c in range(spans):
        both = (early[c] + late[c]).astype(BF)
        usable = lax.broadcasted_iota(jnp.int32, (span_len, both.shape[1]), 1) < counts[c] * DH
        for h in range(2):
            at = slice(c * span_len, (c + 1) * span_len)
            keys = both[h * DH : (h + 1) * DH]
            head_values = both[(2 + h) * DH : (3 + h) * DH]
            scores = jnp.dot(
                query[at, h * DH : (h + 1) * DH], keys, preferred_element_type=F32
            ) / math.sqrt(DH)
            scores = jnp.where(usable, scores, -1e30)
            exponent = jnp.exp(scores - jnp.max(scores, axis=1, keepdims=True))
            share = (exponent / jnp.sum(exponent, axis=1, keepdims=True)).astype(BF)
            result = lax.dot_general(share, head_values, NT, preferred_element_type=F32)
            out[at, h * DH : (h + 1) * DH] = result.astype(BF)
    send[...] = out[...]


def decode(part, order, ranges, counts, query, early, product, pieces):
    tokens, width = query.shape
    spans = counts.shape[0]
    pieces = [pltpu.with_memory_space_constraint(w, pltpu.HBM) for w in pieces]
    shape = jax.ShapeDtypeStruct((tokens, width), BF)
    return pl.pallas_call(
        functools.partial(decode_kernel, part, order, ranges),
        out_shape=(shape, shape),
        in_specs=[SMEM, VMEM, VMEM] + [HBM] * (1 + len(pieces)),
        out_specs=(VMEM, VMEM),
        scratch_shapes=scratch(spans, tokens, order, ranges, product, pieces),
        compiler_params=params(),
    )(counts, query, early, product, *pieces)


def partial_kernel(place, attended, near, grad, near_grad, out):
    left = jnp.concatenate([attended[...], near[...]], axis=0).T
    width = out.shape[2]

    def block(p):
        at = pl.ds(pl.multiple_of((2 * p + place[1]) * width, width), width)
        return jnp.concatenate([grad[:, at], near_grad[:, at]], axis=0)

    for p in range(0, out.shape[0], 2):
        right = jnp.concatenate([block(p), block(p + 1)], axis=1)
        term = jnp.dot(left, right, preferred_element_type=F32).astype(BF)
        out[p] = term[:, :width]
        out[p + 1] = term[:, width:]


def partial_grad(place, attended, near, grad, near_grad, chips):
    return pl.pallas_call(
        partial_kernel,
        out_shape=jax.ShapeDtypeStruct(
            (chips, attended.shape[1], grad.shape[1] // (2 * chips)), BF
        ),
        in_specs=[SMEM, VMEM, VMEM, VMEM, VMEM],
        out_specs=VMEM,
        compiler_params=params(),
    )(place, attended, near, grad, near_grad)


def total_kernel(parts, out):
    total = parts[0].astype(F32)
    for p in range(1, parts.shape[0]):
        total += parts[p].astype(F32)
    out[...] = total


def total_grad(parts):
    return pl.pallas_call(
        total_kernel,
        out_shape=jax.ShapeDtypeStruct(parts.shape[1:], F32),
        in_specs=[VMEM],
        out_specs=VMEM,
        compiler_params=params(),
    )(parts)


def shift(x, axis, step):
    n = lax.axis_size(axis)
    return lax.ppermute(x, axis, [(i, (i + step) % n) for i in range(n)])


def sibling(x):
    return lax.ppermute(x, "core", [(0, 1), (1, 0)])


def exchange_over(x, axis):
    return lax.all_to_all(x, axis, split_axis=0, concat_axis=0, tiled=True)


def exchange(x):
    return lax.all_to_all(x, SEQ, split_axis=0, concat_axis=0, tiled=True)


def local(
    span_states, dec_query, nbr_query, nbr_index, nbr_count, wkv_enc, wo_enc, wkv_dec, grad_out
):
    chips = lax.axis_size("chip")
    devices = 2 * chips
    groups = lax.axis_size("mp")
    chip, core, z = lax.axis_index("chip"), lax.axis_index("core"), lax.axis_index("mp")
    place = jnp.stack([z, core]).astype(jnp.int32)
    spans = nbr_count.shape[0]
    rows = nbr_query.shape[0]
    hidden = span_states.shape[1]

    def ring(x, forward):
        up = [x]
        down = [x]
        for _ in range(3):
            up.append(shift(up[-1], "mp", -1))
            down.append(shift(down[-1], "mp", 1))
        last = shift(up[-1], "mp", -1) if forward else shift(down[-1], "mp", 1)
        return up + [last] + down[:0:-1]

    tags = exchange(make_tags(rows, nbr_index, devices))

    part = 2 * DH // chips
    wo_rows = lax.dynamic_slice_in_dim(wo_enc, chip * part, part, 0)
    tags, wo_rows = lax.optimization_barrier((tags, wo_rows))

    box = outbox(tags, nbr_query, devices)
    box, wkv_dec, wo_rows, wkv_enc = lax.optimization_barrier((box, wkv_dec, wo_rows, wkv_enc))
    inbox = exchange(box)

    pairs = jnp.dot(
        span_states, wkv_enc.reshape(hidden, -1), preferred_element_type=F32
    ).astype(BF)
    wo_rows = ring(wo_rows, True)
    product = multiply(place, wkv_dec.reshape(hidden, -1), wo_rows, devices)
    grad_near = sibling(grad_out)
    inbox, product, grad_near, pairs = lax.optimization_barrier(
        (inbox, product, grad_near, pairs)
    )

    w0, w1 = encode(nbr_index, inbox, pairs)
    product = exchange(product).reshape((chips, 2) + product.shape[1:])

    up, down = [[w0, w1]], [[w0, w1]]
    for _ in range(3):
        up.append([shift(w, "mp", -1) for w in up[-1]])
        down.append([shift(w, "mp", 1) for w in down[-1]])
    last = [shift(up[3][0], "mp", -1), shift(down[3][1], "mp", 1)]
    pieces = [[w0, w1]] + [side for step in zip(up[1:], down[1:]) for side in step] + [last]
    pieces = [w for pair in pieces for w in pair]
    tokens = dec_query.shape[0]
    early = begin(
        spans,
        tokens,
        part,
        (0, 1, groups - 1, 2, groups - 2),
        ((0, 3), (groups - 2, groups)),
        product,
        pieces[:10],
    )
    attended, send = decode(
        part,
        (3, groups - 3, 4),
        ((3, groups - 2),),
        nbr_count,
        dec_query,
        early,
        product,
        pieces[10:],
    )

    near = sibling(send)
    parts = partial_grad(place, send, near, grad_out, grad_near, chips)
    parts = exchange_over(parts, "chip")
    return attended, total_grad(parts)


def solution(mesh):
    devices = mesh.devices
    fine = Mesh(devices.reshape(-1, 2, devices.shape[1]), SEQ + ("mp",))
    return jax.shard_map(
        local,
        mesh=fine,
        in_specs=(
            P(SEQ, None),
            P(SEQ, "mp"),
            P(SEQ, None, "mp"),
            P(SEQ, None),
            P(SEQ),
            P(None, None, "mp"),
            P("mp", None),
            P(None, None, "mp"),
            P(SEQ, None),
        ),
        out_specs=(P(SEQ, "mp"), P("mp", SEQ)),
        check_vma=False,
    )
```

```python
import functools
import math

import jax
import jax.numpy as jnp
from jax import lax
from jax.experimental import pallas as pl
from jax.experimental.pallas import tpu as pltpu
from jax.sharding import Mesh, PartitionSpec as P

DH = 128
BF = jnp.bfloat16
F32 = jnp.float32
VMEM = pl.BlockSpec(memory_space=pltpu.VMEM)
SMEM = pl.BlockSpec(memory_space=pltpu.SMEM)
HBM = pl.BlockSpec(memory_space=pltpu.HBM)
SEQ = ("chip", "core")
ANY = pl.BlockSpec(memory_space=pl.ANY)
NT = (((1,), (1,)), ((), ()))


def params(mebibytes=16):
    return pltpu.CompilerParams(vmem_limit_bytes=mebibytes * 1024 * 1024)


def tags_kernel(rows, index, out):
    spans, slots = index.shape
    for dest in range(out.shape[0]):
        out[dest, 0, 0] = 0
    for j in range(spans * slots):
        entry = index[j // slots, j % slots]
        out[entry // rows, 0, 0] = entry % rows + 1


def make_tags(rows, index, devices):
    return pl.pallas_call(
        functools.partial(tags_kernel, rows),
        out_shape=jax.ShapeDtypeStruct((devices, 1, 1), jnp.int32),
        in_specs=[SMEM],
        out_specs=SMEM,
    )(index)


def product_kernel(place, matrix, *refs):
    pieces, (out, left, result, sems) = refs[:-4], refs[-4:]
    part = left.shape[0] // len(pieces)
    for i, p in enumerate(pieces):
        left[i * part : (i + 1) * part] = p[...]
    first = pl.multiple_of(place[1] * 2 * DH, 2 * DH)
    right = matrix[:, pl.ds(first, 2 * DH)]
    result[...] = jnp.dot(left[...], right, preferred_element_type=F32).astype(BF)
    copies = [
        pltpu.make_async_copy(result, out.at[p], sems.at[p]) for p in range(out.shape[0])
    ]
    for copy in copies:
        copy.start()
    for copy in copies:
        copy.wait()


def multiply(place, matrix, pieces, copies):
    rows = len(pieces) * pieces[0].shape[0]
    return pl.pallas_call(
        product_kernel,
        out_shape=pltpu.HBM((copies, rows, 2 * DH), BF),
        in_specs=[SMEM, VMEM] + [VMEM] * len(pieces),
        out_specs=HBM,
        scratch_shapes=[
            pltpu.VMEM((rows, pieces[0].shape[1]), BF),
            pltpu.VMEM((rows, 2 * DH), BF),
            pltpu.SemaphoreType.DMA((max(copies, len(pieces)),)),
        ],
        compiler_params=params(),
    )(place, matrix, *pieces)


def outbox_kernel(tags, query, out, sems):
    count = out.shape[0]

    def copy(dest):
        return pltpu.make_async_copy(query.at[tags[dest, 0, 0] - 1], out.at[dest], sems.at[dest])

    for dest in range(count):

        @pl.when(tags[dest, 0, 0] > 0)
        def _():
            copy(dest).start()

    for dest in range(count):

        @pl.when(tags[dest, 0, 0] > 0)
        def _():
            copy(dest).wait()


def outbox(tags, query, buckets):
    return pl.pallas_call(
        outbox_kernel,
        out_shape=jax.ShapeDtypeStruct((buckets,) + query.shape[1:], BF),
        in_specs=[SMEM, VMEM],
        out_specs=HBM,
        scratch_shapes=[pltpu.SemaphoreType.DMA((buckets,))],
        compiler_params=params(60),
    )(tags, query)


def encode_kernel(rows, index, inbox, pairs, out0, out1, held, sems):
    spans, slots = index.shape
    span_len = pairs.shape[0] // spans
    copies = []
    for j in range(spans * slots):
        home = index[j // slots, j % slots] // rows
        copies.append(pltpu.make_async_copy(inbox.at[home], held.at[j], sems.at[j]))
        copies[-1].start()
    for c in range(spans):
        for j in range(c * slots, (c + 1) * slots):
            copies[j].wait()
        for head, out in enumerate((out0, out1)):
            at = slice(head * DH, (head + 1) * DH)
            keys = pairs[c * span_len : (c + 1) * span_len, at]
            queries = held[c * slots : (c + 1) * slots, :, at].reshape(-1, DH)
            scores = lax.dot_general(
                keys, queries, NT, preferred_element_type=F32
            ) / math.sqrt(DH)
            exponent = jnp.exp(scores - jnp.max(scores, axis=0, keepdims=True))
            weights = exponent / jnp.sum(exponent, axis=0, keepdims=True)
            out[c * span_len : (c + 1) * span_len] = weights.astype(BF)
    tokens = pairs.shape[0]
    rows = tokens // slots
    for head, out in enumerate((out0, out1)):
        values = pairs[:, (2 + head) * DH : (3 + head) * DH]
        out[tokens:] = jnp.concatenate(
            [values[k * rows : (k + 1) * rows] for k in range(slots)], axis=1
        )


def encode(index, inbox, pairs):
    spans, slots = index.shape
    tokens = pairs.shape[0]
    shape = jax.ShapeDtypeStruct((tokens + tokens // slots, slots * inbox.shape[1]), BF)
    return pl.pallas_call(
        functools.partial(encode_kernel, spans * slots),
        out_shape=(shape, shape),
        in_specs=[SMEM, HBM, VMEM],
        out_specs=(VMEM, VMEM),
        scratch_shapes=[
            pltpu.VMEM((spans * slots,) + inbox.shape[1:], BF),
            pltpu.SemaphoreType.DMA((spans * slots,)),
        ],
        compiler_params=params(),
    )(index, inbox, pairs)


def project(part, order, ranges, product, sources, folded, held, pieces, sems):
    spans = folded.shape[0]
    span_len = folded.shape[2] // (2 * len(order))
    tokens = spans * span_len
    slots = pieces.shape[2] // DH
    arrive = [
        pltpu.make_async_copy(piece, pieces.at[i], sems.at[i])
        for i, piece in enumerate(sources)
    ]
    copies = []
    for k in range(2):
        for first, last in ranges:
            rows = pl.ds(first * part, (last - first) * part)
            copies.append(
                pltpu.make_async_copy(
                    product.at[:, k, rows],
                    held.at[k, :, rows],
                    sems.at[len(arrive) + len(copies)],
                )
            )
    each = len(ranges)
    for copy in copies[:each] + arrive + copies[each:]:
        copy.start()

    def riding(i):
        rows = pieces[i][tokens:]
        return jnp.concatenate([rows[:, k * DH : (k + 1) * DH] for k in range(slots)], axis=0)

    for k in range(2):
        for copy in copies[k * each : (k + 1) * each]:
            copy.wait()
        for n, g in enumerate(order):
            if k == 0:
                arrive[2 * n].wait()
                arrive[2 * n + 1].wait()
            at = slice(g * part, (g + 1) * part)
            rows = jnp.concatenate([held[k, p, at] for p in range(held.shape[1])], axis=0)
            low = jnp.dot(riding(2 * n), rows[:DH], preferred_element_type=F32)
            high = jnp.dot(riding(2 * n + 1), rows[DH:], preferred_element_type=F32)
            for c in range(spans):
                span = slice(c * span_len, (c + 1) * span_len)
                both = jnp.concatenate([low[span], high[span]], axis=0).astype(BF)
                columns = slice(n * 2 * span_len, (n + 1) * 2 * span_len)
                folded[c, k * 2 * DH : (k + 1) * 2 * DH, columns] = both.T
    result = []
    for c in range(spans):
        weights = pieces[:, c * span_len : (c + 1) * span_len].reshape(-1, slots * DH)
        result.append(jnp.dot(folded[c], weights, preferred_element_type=F32))
    return result


def scratch(spans, tokens, order, ranges, product, pieces):
    return [
        pltpu.VMEM((spans, 4 * DH, 2 * len(order) * tokens // spans), BF),
        pltpu.VMEM((2, product.shape[0]) + product.shape[2:], BF),
        pltpu.VMEM((len(pieces),) + pieces[0].shape, BF),
        pltpu.SemaphoreType.DMA((len(pieces) + 2 * len(ranges),)),
    ]


def begin_kernel(part, order, ranges, product, *refs):
    out, folded, held, pieces, sems = refs[-5:]
    for c, both in enumerate(
        project(part, order, ranges, product, refs[:-5], folded, held, pieces, sems)
    ):
        out[c] = both


def begin(spans, tokens, part, order, ranges, product, pieces):
    pieces = [pltpu.with_memory_space_constraint(w, pltpu.HBM) for w in pieces]
    return pl.pallas_call(
        functools.partial(begin_kernel, part, order, ranges),
        out_shape=jax.ShapeDtypeStruct((spans, 4 * DH, pieces[0].shape[1]), F32),
        in_specs=[HBM] * (1 + len(pieces)),
        out_specs=VMEM,
        scratch_shapes=scratch(spans, tokens, order, ranges, product, pieces),
        compiler_params=params(),
    )(product, *pieces)


def decode_kernel(part, order, ranges, counts, query, early, product, *refs):
    out, send, folded, held, pieces, sems = refs[-6:]
    spans = folded.shape[0]
    span_len = query.shape[0] // spans
    late = project(part, order, ranges, product, refs[:-6], folded, held, pieces, sems)
    for c in range(spans):
        both = (early[c] + late[c]).astype(BF)
        usable = lax.broadcasted_iota(jnp.int32, (span_len, both.shape[1]), 1) < counts[c] * DH
        for h in range(2):
            at = slice(c * span_len, (c + 1) * span_len)
            keys = both[h * DH : (h + 1) * DH]
            head_values = both[(2 + h) * DH : (3 + h) * DH]
            scores = jnp.dot(
                query[at, h * DH : (h + 1) * DH], keys, preferred_element_type=F32
            ) / math.sqrt(DH)
            scores = jnp.where(usable, scores, -1e30)
            exponent = jnp.exp(scores - jnp.max(scores, axis=1, keepdims=True))
            share = (exponent / jnp.sum(exponent, axis=1, keepdims=True)).astype(BF)
            result = lax.dot_general(share, head_values, NT, preferred_element_type=F32)
            out[at, h * DH : (h + 1) * DH] = result.astype(BF)
    send[...] = out[...]


def decode(part, order, ranges, counts, query, early, product, pieces):
    tokens, width = query.shape
    spans = counts.shape[0]
    pieces = [pltpu.with_memory_space_constraint(w, pltpu.HBM) for w in pieces]
    shape = jax.ShapeDtypeStruct((tokens, width), BF)
    return pl.pallas_call(
        functools.partial(decode_kernel, part, order, ranges),
        out_shape=(shape, shape),
        in_specs=[SMEM, VMEM, VMEM] + [HBM] * (1 + len(pieces)),
        out_specs=(VMEM, VMEM),
        scratch_shapes=scratch(spans, tokens, order, ranges, product, pieces),
        compiler_params=params(),
    )(counts, query, early, product, *pieces)


def partial_kernel(place, attended, near, grad, near_grad, out):
    left = jnp.concatenate([attended[...], near[...]], axis=0).T
    width = out.shape[2]

    def block(p):
        at = pl.ds(pl.multiple_of((2 * p + place[1]) * width, width), width)
        return jnp.concatenate([grad[:, at], near_grad[:, at]], axis=0)

    for p in range(0, out.shape[0], 2):
        right = jnp.concatenate([block(p), block(p + 1)], axis=1)
        term = jnp.dot(left, right, preferred_element_type=F32).astype(BF)
        out[p] = term[:, :width]
        out[p + 1] = term[:, width:]


def partial_grad(place, attended, near, grad, near_grad, chips):
    return pl.pallas_call(
        partial_kernel,
        out_shape=jax.ShapeDtypeStruct(
            (chips, attended.shape[1], grad.shape[1] // (2 * chips)), BF
        ),
        in_specs=[SMEM, VMEM, VMEM, VMEM, VMEM],
        out_specs=VMEM,
        compiler_params=params(),
    )(place, attended, near, grad, near_grad)


def total_kernel(parts, out):
    total = parts[0].astype(F32)
    for p in range(1, parts.shape[0]):
        total += parts[p].astype(F32)
    out[...] = total


def total_grad(parts):
    return pl.pallas_call(
        total_kernel,
        out_shape=jax.ShapeDtypeStruct(parts.shape[1:], F32),
        in_specs=[VMEM],
        out_specs=VMEM,
        compiler_params=params(),
    )(parts)


def shift(x, axis, step):
    n = lax.axis_size(axis)
    return lax.ppermute(x, axis, [(i, (i + step) % n) for i in range(n)])


def sibling(x):
    return lax.ppermute(x, "core", [(0, 1), (1, 0)])


def exchange_over(x, axis):
    return lax.all_to_all(x, axis, split_axis=0, concat_axis=0, tiled=True)


def exchange(x):
    return lax.all_to_all(x, SEQ, split_axis=0, concat_axis=0, tiled=True)


def local(
    span_states, dec_query, nbr_query, nbr_index, nbr_count, wkv_enc, wo_enc, wkv_dec, grad_out
):
    chips = lax.axis_size("chip")
    devices = 2 * chips
    groups = lax.axis_size("mp")
    chip, core, z = lax.axis_index("chip"), lax.axis_index("core"), lax.axis_index("mp")
    place = jnp.stack([z, core]).astype(jnp.int32)
    spans = nbr_count.shape[0]
    rows = nbr_query.shape[0]
    hidden = span_states.shape[1]

    def ring(x, forward):
        up = [x]
        down = [x]
        for _ in range(3):
            up.append(shift(up[-1], "mp", -1))
            down.append(shift(down[-1], "mp", 1))
        last = shift(up[-1], "mp", -1) if forward else shift(down[-1], "mp", 1)
        return up + [last] + down[:0:-1]

    tags = exchange(make_tags(rows, nbr_index, devices))

    part = 2 * DH // chips
    wo_rows = lax.dynamic_slice_in_dim(wo_enc, chip * part, part, 0)
    tags, wo_rows = lax.optimization_barrier((tags, wo_rows))

    box = outbox(tags, nbr_query, devices)
    box, wkv_dec, wo_rows, wkv_enc = lax.optimization_barrier((box, wkv_dec, wo_rows, wkv_enc))
    inbox = exchange(box)

    pairs = jnp.dot(
        span_states, wkv_enc.reshape(hidden, -1), preferred_element_type=F32
    ).astype(BF)
    wo_rows = ring(wo_rows, True)
    product = multiply(place, wkv_dec.reshape(hidden, -1), wo_rows, devices)
    grad_near = sibling(grad_out)
    inbox, product, grad_near, pairs = lax.optimization_barrier(
        (inbox, product, grad_near, pairs)
    )

    w0, w1 = encode(nbr_index, inbox, pairs)
    product = exchange(product).reshape((chips, 2) + product.shape[1:])

    up, down = [[w0, w1]], [[w0, w1]]
    for _ in range(3):
        up.append([shift(w, "mp", -1) for w in up[-1]])
        down.append([shift(w, "mp", 1) for w in down[-1]])
    last = [shift(up[3][0], "mp", -1), shift(down[3][1], "mp", 1)]
    pieces = [[w0, w1]] + [side for step in zip(up[1:], down[1:]) for side in step] + [last]
    pieces = [w for pair in pieces for w in pair]
    tokens = dec_query.shape[0]
    early = begin(
        spans,
        tokens,
        part,
        (0, 1, groups - 1, 2, groups - 2),
        ((0, 3), (groups - 2, groups)),
        product,
        pieces[:10],
    )
    attended, send = decode(
        part,
        (3, groups - 3, 4),
        ((3, groups - 2),),
        nbr_count,
        dec_query,
        early,
        product,
        pieces[10:],
    )

    near = sibling(send)
    parts = partial_grad(place, send, near, grad_out, grad_near, chips)
    parts = exchange_over(parts, "chip")
    return attended, total_grad(parts)


def solution(mesh):
    devices = mesh.devices
    fine = Mesh(devices.reshape(-1, 2, devices.shape[1]), SEQ + ("mp",))
    return jax.shard_map(
        local,
        mesh=fine,
        in_specs=(
            P(SEQ, None),
            P(SEQ, "mp"),
            P(SEQ, None, "mp"),
            P(SEQ, None),
            P(SEQ),
            P(None, None, "mp"),
            P("mp", None),
            P(None, None, "mp"),
            P(SEQ, None),
        ),
        out_specs=(P(SEQ, "mp"), P("mp", SEQ)),
        check_vma=False,
    )
```
